512 devices in a mesh: doc: 4 (over x), seq: 128 (over y, z, core).
Axes of the slice: x: 4, y: 8, z: 8, core: 2. Of those that a mesh axis runs over, the one named last changes fastest.
Arguments:
- hidden_rows: bfloat16 [262144, 2048], P(('doc', 'seq')), parts along dimension 0, may hold values from -24 to 24
- w_expand: bfloat16 [2048, 8192], P(None, 'seq'), may hold values from -0.125 to 0.125
- w_contract: bfloat16 [8192, 2048], P('seq'), may hold values from -0.25 to 0.25
Outputs:
- short_out: bfloat16 [1024, 2048], P('doc', 'seq'), parts along dimension 0
The draws below stay inside these ranges and needn't reach their ends.
There are 4 independent parts, one for each index of `doc`. The reference program is written for one: setup_inputs(seed, part) draws one part's arguments, and reference() takes and returns one part's arrays. A program takes and returns all parts, laid end to end along the dimension named above; an argument that names none is the same for every part. Nothing has to cross between parts.
All inputs are finite; a program needn't handle non-finite values.
Results may differ from the reference program's by a relative error of at most 0.0057.
Values may be sent and summed in bfloat16 or wider, within the bound.
No kernel may reach another device: no remote copies, remote signals or barrier semaphores. Data moves between devices by JAX's collectives and lax.ppermute only.
A program may use at most 64 MiB of HBM per device.

```python
import math
import jax
import jax.numpy as jnp
from jax import lax

D = 2048
FF = 8192
KEEP = 256
SEQ = 65536


def raised(array, key, source, target, blocks, factor):
    owner, partner = [(jnp.arange(array.shape[position]) // (array.shape[position] // blocks)).reshape([-1 if axis == position else 1 for axis in range(array.ndim)]) for position in (source, target)]
    chosen = jax.random.permutation(key, blocks)[partner]
    strong = (owner == chosen) | (owner == (partner + blocks // 2) % blocks)
    return jnp.where(strong, factor * array, array)


def level_of(own_key, dims, shards, least, high):
    level, own = 1.0, jax.random.fold_in(own_key, 6)
    for axis_at, parts in shards:
        draws = jnp.exp(jax.random.uniform(jax.random.fold_in(own, axis_at), (parts,), jnp.float32, least / len(shards), high / len(shards)))
        level = level * jnp.repeat(draws, dims[axis_at] // parts).reshape([-1 if axis == axis_at else 1 for axis in range(len(dims))])
    return level


def gaussian(key, extent, spread, reach, split=(), kind=jnp.bfloat16):
    array = jax.random.normal(key, extent, jnp.float32) * spread
    if len(split) > 0:
        array = level_of(key, extent, split, -0.22, 0.18) * array
    return jnp.clip(array, min=-reach, max=reach).astype(kind)


def noise_with(key, extent, width, bound, cuts, heavy, kind=jnp.bfloat16):
    values = width * jax.random.normal(key, extent, jnp.float32)
    if cuts:
        values = values * level_of(key, extent, cuts, -0.22, 0.18)
    return jnp.clip(raised(values, jax.random.fold_in(key, 3), *heavy), -bound, bound).astype(kind)


def setup_inputs(seed: int = 0, part: int = 0) -> dict:
    key_of = jax.random.split(jax.random.key(seed), 4)
    part_splits = jax.random.split(jax.random.fold_in(key_of[3], part), 4)
    return {
        "hidden_rows": noise_with(part_splits[0], (SEQ, D), 1.0, 24.0, ((0, 128),), (0, 1, 128, 5.5)),
        "w_expand": gaussian(key_of[1], (D, FF), D ** -0.5, 0.125, ((1, 128),)),
        "w_contract": noise_with(key_of[2], (FF, D), FF ** -0.5, 0.25, ((0, 128),), (0, 1, 128, 5.5)),
    }


def cosine_table(first_row, count, seq_len, keep):
    freq = jnp.arange(keep, dtype=jnp.int32)
    posit = first_row + jnp.arange(count, dtype=jnp.int32)
    phase = (2 * posit[None, :] + 1) * freq[:, None] % (4 * seq_len)
    return jnp.cos(phase.astype(jnp.float32) * (math.pi / (2.0 * seq_len))).astype(jnp.bfloat16)

def reference(hidden_rows, w_expand, w_contract):
    table = cosine_table(0, SEQ, SEQ, KEEP)
    coeffs = (math.sqrt(2.0 / SEQ) * jnp.dot(table, hidden_rows, preferred_element_type=jnp.float32)).astype(jnp.bfloat16)
    wide = coeffs.astype(jnp.float32)
    scale = lax.rsqrt(lax.optimization_barrier(jnp.mean(wide * wide, axis=1)) + 1e-06)
    expanded = jnp.dot(coeffs, w_expand, preferred_element_type=jnp.float32) * scale[:, None]
    activated = jax.nn.gelu(expanded).astype(jnp.bfloat16)
    branch = jnp.dot(activated, w_contract, preferred_element_type=jnp.float32)
    return (wide + branch).astype(jnp.bfloat16)
```

```python
import math

import jax
import jax.numpy as jnp
import numpy as np
from jax import lax
from jax.experimental import pallas as pl
from jax.experimental.pallas import tpu as pltpu
from jax.sharding import PartitionSpec as P

KEEP = 256
MOMENTS = 16
F32, BF16 = jnp.float32, jnp.bfloat16


def split_halves(array):
    high = np.asarray(array, np.float32).astype(jnp.bfloat16)
    low = (np.asarray(array, np.float64) - high.astype(np.float64)).astype(jnp.bfloat16)
    return high, low


def window_tables(rows, windows):
    t = (2.0 * np.arange(rows) + 1.0 - rows) / rows
    basis, _ = np.linalg.qr(np.polynomial.chebyshev.chebvander(t, MOMENTS - 1))
    basis = basis[:, list(range(0, MOMENTS, 2)) + list(range(1, MOMENTS, 2))]
    k = np.arange(KEEP)
    inner = np.pi * np.outer(k, t) / (2 * windows)
    norm = math.sqrt(2.0 / (rows * windows))
    even = norm * np.cos(inner) @ basis[:, : MOMENTS // 2]
    odd = -norm * np.sin(inner) @ basis[:, MOMENTS // 2 :]
    expand = np.concatenate([even, odd], axis=1).T.astype(np.float32)
    high, low = split_halves(basis.T)
    project = np.concatenate([high, low], axis=0)
    theta = np.pi * np.outer(2 * np.arange(windows) + 1, k) / (2 * windows)
    trig = np.concatenate([np.cos(theta), np.sin(theta)], axis=1)
    trig = trig.reshape(windows // 2, 2, 2 * KEEP).transpose(1, 0, 2)
    high, low = split_halves(trig)
    return project, expand, np.concatenate([high, low, high, low], axis=1)


def moments_kernel(project_ref, rows_ref, out_ref):
    both = jnp.dot(project_ref[...], rows_ref[...], preferred_element_type=F32)
    moments = both[:MOMENTS] + both[MOMENTS:]
    copies = jnp.concatenate([moments] * 8, axis=0)
    row = lax.broadcasted_iota(jnp.int32, (128, 128), 0) % 8
    lane = lax.broadcasted_iota(jnp.int32, (128, 128), 1) // MOMENTS
    for block in range(moments.shape[1] // 128):
        turned = copies[:, 128 * block : 128 * (block + 1)].T
        packed = jnp.where(row == lane, turned, 0.0).reshape(16, 8, 128).sum(axis=1)
        out_ref[16 * block : 16 * (block + 1), :] = packed


def coeffs_kernel(core_ref, moments_ref, trig_ref, expand_ref, out_ref):
    trig = trig_ref[0]
    sources = trig.shape[0] // 4
    expand = expand_ref[...]
    half = MOMENTS // 2
    for part in range(4):
        rows = moments_ref[pl.ds(part, sources, stride=4), :]
        high = rows.astype(BF16)
        low = (rows - high.astype(F32)).astype(BF16)
        stacked = jnp.concatenate([high, high, low, low], axis=0)
        turned = lax.dot_general(stacked, trig, (((0,), (0,)), ((), ())), preferred_element_type=F32)
        even = turned[:, :KEEP].reshape(8, MOMENTS, KEEP)[:, :half]
        odd = turned[:, KEEP:].reshape(8, MOMENTS, KEEP)[:, half:]
        out_ref[8 * part : 8 * (part + 1), :] = (even * expand[:half] + odd * expand[half:]).sum(axis=1)


def feed_forward_kernel(coeffs_ref, expand_ref, contract_ref, out_ref):
    coeffs = coeffs_ref[...]
    wide = coeffs.astype(F32)
    scale = lax.rsqrt(jnp.sum(wide * wide, axis=0, keepdims=True) / coeffs.shape[0] + 1e-06)
    expanded = jnp.dot(expand_ref[...], coeffs, preferred_element_type=F32) * scale
    activated = jax.nn.gelu(expanded).astype(BF16)
    branch = lax.dot_general(contract_ref[...], activated, (((0,), (0,)), ((), ())), preferred_element_type=F32)
    out_ref[...] = branch.astype(BF16)


def add_kernel(parts_ref, coeffs_ref, out_ref):
    total = jnp.sum(parts_ref[...].astype(F32), axis=0)
    out_ref[...] = (coeffs_ref[...].astype(F32) + total).astype(BF16)


def local(hidden_rows, w_expand, w_contract):
    rows, width = hidden_rows.shape
    windows = lax.axis_size("seq")
    chips = windows // 2
    mine = width // chips
    project, expand, trig = window_tables(rows, windows)
    same_core = [list(range(core, windows, 2)) for core in range(2)]
    pairs = [[2 * chip, 2 * chip + 1] for chip in range(chips)]
    core = lax.axis_index("seq") % 2

    def exchange(x):
        return lax.all_to_all(x, "seq", 0, 0, axis_index_groups=same_core)

    def gather_pair(x):
        return lax.all_gather(x, "seq", axis_index_groups=pairs)

    units_in = gather_pair(w_expand.T).reshape(-1, width)
    units_out = gather_pair(w_contract).reshape(-1, width)

    steps = 4
    moments = pl.pallas_call(
        moments_kernel,
        grid=(steps,),
        in_specs=[
            pl.BlockSpec((2 * MOMENTS, rows), lambda i: (0, 0)),
            pl.BlockSpec((rows, width // steps), lambda i: (0, i)),
        ],
        out_specs=pl.BlockSpec((width // 8 // steps, 128), lambda i: (i, 0)),
        out_shape=jax.ShapeDtypeStruct((width // 8, 128), F32),
    )(jnp.asarray(project), hidden_rows)
    received = exchange(moments.reshape(chips, -1, 128)).reshape(-1, 128)
    partial = pl.pallas_call(
        coeffs_kernel,
        grid_spec=pltpu.PrefetchScalarGridSpec(
            num_scalar_prefetch=1,
            grid=(1,),
            in_specs=[
                pl.BlockSpec(received.shape, lambda i, core: (0, 0)),
                pl.BlockSpec((1,) + trig.shape[1:], lambda i, core: (core[0], 0, 0)),
                pl.BlockSpec(expand.shape, lambda i, core: (0, 0)),
            ],
            out_specs=pl.BlockSpec((mine, KEEP), lambda i, core: (0, 0)),
        ),
        out_shape=jax.ShapeDtypeStruct((mine, KEEP), F32),
    )(core.astype(jnp.int32).reshape(1), received, jnp.asarray(trig), jnp.asarray(expand))
    both = gather_pair(partial)
    coeffs = (both[0] + both[1]).astype(BF16)
    coeffs = jnp.where(core == 0, coeffs[:, : KEEP // 2], coeffs[:, KEEP // 2 :])
    spread = exchange(jnp.broadcast_to(coeffs[None], (chips,) + coeffs.shape)).reshape(width, -1)
    branch = pl.pallas_call(
        feed_forward_kernel,
        out_shape=jax.ShapeDtypeStruct(spread.shape, BF16),
    )(spread, units_in, units_out)
    parts = exchange(branch.reshape(chips, mine, -1))
    result = pl.pallas_call(
        add_kernel,
        out_shape=jax.ShapeDtypeStruct(coeffs.shape, BF16),
    )(parts, coeffs)
    halves = gather_pair(result)
    halves = jnp.where(core == 0, halves[:, : mine // 2], halves[:, mine // 2 :])
    return jnp.transpose(halves, (0, 2, 1)).reshape(KEEP, mine // 2)


def solution(mesh):
    return jax.shard_map(
        local,
        mesh=mesh,
        in_specs=(P(("doc", "seq"), None), P(None, "seq"), P("seq", None)),
        out_specs=P("doc", "seq"),
        check_vma=False,
    )
```

```python
import math

import jax
import jax.numpy as jnp
import numpy as np
from jax import lax
from jax.experimental import pallas as pl
from jax.experimental.pallas import tpu as pltpu
from jax.sharding import PartitionSpec as P

KEEP = 256
MOMENTS = 16
F32, BF16 = jnp.float32, jnp.bfloat16


def split_halves(array):
    high = np.asarray(array, np.float32).astype(jnp.bfloat16)
    low = (np.asarray(array, np.float64) - high.astype(np.float64)).astype(jnp.bfloat16)
    return high, low


def window_tables(rows, windows):
    t = (2.0 * np.arange(rows) + 1.0 - rows) / rows
    basis, _ = np.linalg.qr(np.polynomial.chebyshev.chebvander(t, MOMENTS - 1))
    basis = basis[:, list(range(0, MOMENTS, 2)) + list(range(1, MOMENTS, 2))]
    k = np.arange(KEEP)
    inner = np.pi * np.outer(k, t) / (2 * windows)
    norm = math.sqrt(2.0 / (rows * windows))
    even = norm * np.cos(inner) @ basis[:, : MOMENTS // 2]
    odd = -norm * np.sin(inner) @ basis[:, MOMENTS // 2 :]
    expand = np.concatenate([even, odd], axis=1).T.astype(np.float32)
    high, low = split_halves(basis.T)
    project = np.concatenate([high, low], axis=0)
    theta = np.pi * np.outer(2 * np.arange(windows) + 1, k) / (2 * windows)
    trig = np.concatenate([np.cos(theta), np.sin(theta)], axis=1)
    trig = trig.reshape(windows // 2, 2, 2 * KEEP).transpose(1, 0, 2)
    high, low = split_halves(trig)
    return project, expand, np.concatenate([high, low, high, low], axis=1)


def moments_kernel(project_ref, rows_ref, out_ref):
    both = jnp.dot(project_ref[...], rows_ref[...], preferred_element_type=F32)
    moments = both[:MOMENTS] + both[MOMENTS:]
    copies = jnp.concatenate([moments] * 8, axis=0)
    row = lax.broadcasted_iota(jnp.int32, (128, 128), 0) % 8
    lane = lax.broadcasted_iota(jnp.int32, (128, 128), 1) // MOMENTS
    for block in range(moments.shape[1] // 128):
        turned = copies[:, 128 * block : 128 * (block + 1)].T
        packed = jnp.where(row == lane, turned, 0.0).reshape(16, 8, 128).sum(axis=1)
        out_ref[16 * block : 16 * (block + 1), :] = packed


def coeffs_kernel(core_ref, moments_ref, trig_ref, expand_ref, out_ref):
    trig = trig_ref[0]
    sources = trig.shape[0] // 4
    expand = expand_ref[...]
    half = MOMENTS // 2
    for part in range(4):
        rows = moments_ref[pl.ds(part, sources, stride=4), :]
        high = rows.astype(BF16)
        low = (rows - high.astype(F32)).astype(BF16)
        stacked = jnp.concatenate([high, high, low, low], axis=0)
        turned = lax.dot_general(stacked, trig, (((0,), (0,)), ((), ())), preferred_element_type=F32)
        even = turned[:, :KEEP].reshape(8, MOMENTS, KEEP)[:, :half]
        odd = turned[:, KEEP:].reshape(8, MOMENTS, KEEP)[:, half:]
        out_ref[8 * part : 8 * (part + 1), :] = (even * expand[:half] + odd * expand[half:]).sum(axis=1)


def spread_kernel(core_ref, both_ref, coeffs_ref, out_ref):
    total = both_ref[0] + both_ref[1]
    half = total.shape[1] // 2
    mine = jnp.where(core_ref[0] == 0, total[:, :half], total[:, half:])
    coeffs_ref[...] = mine.astype(BF16)
    low, high = mine[:16], mine[16:]
    left = lax.broadcasted_iota(jnp.int32, low.shape, 1) < half // 2
    first = jnp.where(left, low, pltpu.roll(high, half // 2, 1)).astype(BF16)
    second = jnp.where(left, pltpu.roll(low, half // 2, 1), high).astype(BF16)
    pair = jnp.stack([first, second])
    out_ref[...] = jnp.broadcast_to(pair[None], (out_ref.shape[0] // 2,) + pair.shape).reshape(out_ref.shape)


def feed_forward_kernel(coeffs_ref, *refs):
    weights, out_ref = refs[:-1], refs[-1]
    units = weights[0].shape[0] // 2
    packed = coeffs_ref[...]
    kept = packed.shape[2] // 2
    width = packed.shape[0] * 32
    coeffs = jnp.concatenate([packed[:, :, :kept], packed[:, :, kept:]], axis=1).reshape(width, kept)
    wide = coeffs.astype(F32)
    scale = lax.rsqrt(jnp.sum(wide * wide, axis=0, keepdims=True) / width + 1e-06)
    branch = jnp.zeros((width, kept), F32)
    for ref in weights:
        expanded = jnp.dot(ref[:units, :], coeffs, preferred_element_type=F32) * scale
        activated = jax.nn.gelu(expanded).astype(BF16)
        branch += lax.dot_general(ref[units:, :], activated, (((0,), (0,)), ((), ())), preferred_element_type=F32)
    parts = branch.reshape(-1, 32, kept)
    out_ref[...] = jnp.concatenate([parts[:, :16], parts[:, 16:]], axis=2).astype(BF16)


def add_kernel(parts_ref, coeffs_ref, out_ref):
    sources, rows, lanes = parts_ref.shape
    sums = jnp.sum(parts_ref[...].astype(F32).reshape(sources // 2, 2, rows, lanes), axis=0)
    first, second = sums[0], sums[1]
    left = lax.broadcasted_iota(jnp.int32, first.shape, 1) < lanes // 2
    low = jnp.where(left, first, pltpu.roll(second, lanes // 2, 1))
    high = jnp.where(left, pltpu.roll(first, lanes // 2, 1), second)
    total = jnp.concatenate([low, high], axis=0)
    out_ref[...] = (coeffs_ref[...].astype(F32) + total).astype(BF16)


def local(hidden_rows, w_expand, w_contract):
    rows, width = hidden_rows.shape
    windows = lax.axis_size("seq")
    chips = windows // 2
    mine = width // chips
    project, expand, trig = window_tables(rows, windows)
    same_core = [list(range(core, windows, 2)) for core in range(2)]
    pairs = [[2 * chip, 2 * chip + 1] for chip in range(chips)]
    core = lax.axis_index("seq") % 2

    def exchange(x):
        return lax.all_to_all(x, "seq", 0, 0, axis_index_groups=same_core)

    def gather_pair(x):
        return lax.all_gather(x, "seq", axis_index_groups=pairs)

    own = jnp.concatenate([w_expand.T, w_contract], axis=0)
    beside = lax.ppermute(own, "seq", [(i, i ^ 2) for i in range(windows)])
    other_core = [(i, i ^ 1) for i in range(windows)]
    weights = [own, beside, lax.ppermute(own, "seq", other_core), lax.ppermute(beside, "seq", other_core)]

    steps = 4
    moments = pl.pallas_call(
        moments_kernel,
        grid=(steps,),
        in_specs=[
            pl.BlockSpec((2 * MOMENTS, rows), lambda i: (0, 0)),
            pl.BlockSpec((rows, width // steps), lambda i: (0, i)),
        ],
        out_specs=pl.BlockSpec((width // 8 // steps, 128), lambda i: (i, 0)),
        out_shape=jax.ShapeDtypeStruct((width // 8, 128), F32),
    )(jnp.asarray(project), hidden_rows)
    received = exchange(moments.reshape(chips, -1, 128)).reshape(-1, 128)
    partial = pl.pallas_call(
        coeffs_kernel,
        grid_spec=pltpu.PrefetchScalarGridSpec(
            num_scalar_prefetch=1,
            grid=(1,),
            in_specs=[
                pl.BlockSpec(received.shape, lambda i, core: (0, 0)),
                pl.BlockSpec((1,) + trig.shape[1:], lambda i, core: (core[0], 0, 0)),
                pl.BlockSpec(expand.shape, lambda i, core: (0, 0)),
            ],
            out_specs=pl.BlockSpec((mine, KEEP), lambda i, core: (0, 0)),
        ),
        out_shape=jax.ShapeDtypeStruct((mine, KEEP), F32),
    )(core.astype(jnp.int32).reshape(1), received, jnp.asarray(trig), jnp.asarray(expand))
    both = gather_pair(partial)
    coeffs, spread = pl.pallas_call(
        spread_kernel,
        grid_spec=pltpu.PrefetchScalarGridSpec(
            num_scalar_prefetch=1,
            grid=(1,),
            in_specs=[pl.BlockSpec(both.shape, lambda i, core: (0, 0, 0))],
            out_specs=[
                pl.BlockSpec((mine, KEEP // 2), lambda i, core: (0, 0)),
                pl.BlockSpec((chips, mine // 2, KEEP // 2), lambda i, core: (0, 0, 0)),
            ],
        ),
        out_shape=[
            jax.ShapeDtypeStruct((mine, KEEP // 2), BF16),
            jax.ShapeDtypeStruct((chips, mine // 2, KEEP // 2), BF16),
        ],
    )(core.astype(jnp.int32).reshape(1), both)
    branch = pl.pallas_call(
        feed_forward_kernel,
        out_shape=jax.ShapeDtypeStruct(spread.shape, BF16),
    )(exchange(spread), *weights)
    result = pl.pallas_call(
        add_kernel,
        out_shape=jax.ShapeDtypeStruct(coeffs.shape, BF16),
    )(exchange(branch), coeffs)
    halves = gather_pair(result)
    halves = jnp.where(core == 0, halves[:, : mine // 2], halves[:, mine // 2 :])
    return jnp.transpose(halves, (0, 2, 1)).reshape(KEEP, mine // 2)


def solution(mesh):
    return jax.shard_map(
        local,
        mesh=mesh,
        in_specs=(P(("doc", "seq"), None), P(None, "seq"), P("seq", None)),
        out_specs=P("doc", "seq"),
        check_vma=False,
    )
```

```python
import math

import jax
import jax.numpy as jnp
import numpy as np
from jax import lax
from jax.experimental import pallas as pl
from jax.experimental.pallas import tpu as pltpu
from jax.sharding import PartitionSpec as P

KEEP = 256
MOMENTS = 16
F32, BF16 = jnp.float32, jnp.bfloat16
VMEM = pl.BlockSpec(memory_space=pltpu.VMEM)
SMEM = pl.BlockSpec(memory_space=pltpu.SMEM)
ANY = pl.BlockSpec(memory_space=pl.ANY)


def split_halves(array):
    high = np.asarray(array, np.float32).astype(jnp.bfloat16)
    low = (np.asarray(array, np.float64) - high.astype(np.float64)).astype(jnp.bfloat16)
    return high, low


def window_tables(rows, windows):
    t = (2.0 * np.arange(rows) + 1.0 - rows) / rows
    basis, _ = np.linalg.qr(np.polynomial.chebyshev.chebvander(t, MOMENTS - 1))
    basis = basis[:, list(range(0, MOMENTS, 2)) + list(range(1, MOMENTS, 2))]
    k = np.arange(KEEP)
    inner = np.pi * np.outer(k, t) / (2 * windows)
    norm = math.sqrt(2.0 / (rows * windows))
    even = norm * np.cos(inner) @ basis[:, : MOMENTS // 2]
    odd = -norm * np.sin(inner) @ basis[:, MOMENTS // 2 :]
    expand = np.concatenate([even, odd], axis=1).T.astype(np.float32)
    high, low = split_halves(basis.T)
    project = np.concatenate([high, low], axis=0)
    theta = np.pi * np.outer(2 * np.arange(windows) + 1, k) / (2 * windows)
    trig = np.concatenate([np.cos(theta), np.sin(theta)], axis=1)
    trig = trig.reshape(windows // 2, 2, 2 * KEEP).transpose(1, 0, 2)
    high, low = split_halves(trig)
    return project, expand, np.concatenate([high, low, high, low], axis=1)


def moments_kernel(project_ref, rows_ref, w_expand_ref, w_contract_ref, out_ref, weights_ref, sems):
    units = w_expand_ref.shape[0]
    copies = [
        pltpu.make_async_copy(w_expand_ref, weights_ref.at[pl.ds(0, units)], sems.at[0]),
        pltpu.make_async_copy(w_contract_ref, weights_ref.at[pl.ds(units, units)], sems.at[1]),
    ]
    for copy in copies:
        copy.start()
    both = jnp.dot(project_ref[...], rows_ref[...], preferred_element_type=F32)
    moments = both[:MOMENTS] + both[MOMENTS:]
    spread = jnp.concatenate([moments] * 8, axis=0)
    row = lax.broadcasted_iota(jnp.int32, (128, 128), 0) % 8
    lane = lax.broadcasted_iota(jnp.int32, (128, 128), 1) // MOMENTS
    for block in range(moments.shape[1] // 128):
        turned = spread[:, 128 * block : 128 * (block + 1)].T
        packed = jnp.where(row == lane, turned, 0.0).reshape(16, 8, 128).sum(axis=1)
        out_ref[16 * block : 16 * (block + 1), :] = packed
    for copy in copies:
        copy.wait()


def coeffs_kernel(core_ref, moments_ref, trig_ref, expand_ref, out_ref):
    trig = trig_ref[core_ref[0]]
    sources = trig.shape[0] // 4
    expand = expand_ref[...]
    half = MOMENTS // 2
    for part in range(4):
        rows = moments_ref[pl.ds(part, sources, stride=4), :]
        high = rows.astype(BF16)
        low = (rows - high.astype(F32)).astype(BF16)
        stacked = jnp.concatenate([high, high, low, low], axis=0)
        turned = lax.dot_general(stacked, trig, (((0,), (0,)), ((), ())), preferred_element_type=F32)
        even = turned[:, :KEEP].reshape(8, MOMENTS, KEEP)[:, :half]
        odd = turned[:, KEEP:].reshape(8, MOMENTS, KEEP)[:, half:]
        out_ref[8 * part : 8 * (part + 1), :] = (even * expand[:half] + odd * expand[half:]).sum(axis=1)


def spread_kernel(core_ref, both_ref, weights_ref, coeffs_ref, out_ref, same_weights_ref):
    total = both_ref[0] + both_ref[1]
    half = total.shape[1] // 2
    mine = jnp.where(core_ref[0] == 0, total[:, :half], total[:, half:])
    coeffs_ref[...] = mine.astype(BF16)
    low, high = mine[:16], mine[16:]
    left = lax.broadcasted_iota(jnp.int32, low.shape, 1) < half // 2
    first = jnp.where(left, low, pltpu.roll(high, half // 2, 1)).astype(BF16)
    second = jnp.where(left, pltpu.roll(low, half // 2, 1), high).astype(BF16)
    pair = jnp.stack([first, second])
    out_ref[...] = jnp.broadcast_to(pair[None], (out_ref.shape[0] // 2,) + pair.shape).reshape(out_ref.shape)


def feed_forward_kernel(coeffs_ref, *refs):
    weights, out_ref = refs[:-1], refs[-1]
    units = weights[0].shape[0] // 2
    packed = coeffs_ref[...]
    kept = packed.shape[2] // 2
    width = packed.shape[0] * 32
    coeffs = jnp.concatenate([packed[:, :, :kept], packed[:, :, kept:]], axis=1).reshape(width, kept)
    wide = coeffs.astype(F32)
    scale = lax.rsqrt(jnp.sum(wide * wide, axis=0, keepdims=True) / width + 1e-06)
    activated = []
    for ref in weights:
        expanded = jnp.dot(ref[:units, :], coeffs, preferred_element_type=F32) * scale
        activated.append(jax.nn.gelu(expanded))
    activated = jnp.concatenate(activated, axis=0).T.astype(BF16)
    contract = jnp.concatenate([ref[units:, :] for ref in weights], axis=0)
    branch = jnp.dot(activated, contract, preferred_element_type=F32)
    for block in range(width // 128):
        turned = branch[:, 128 * block : 128 * (block + 1)].T.reshape(4, 32, kept)
        out_ref[4 * block : 4 * (block + 1)] = jnp.concatenate([turned[:, :16], turned[:, 16:]], axis=2).astype(BF16)


def add_kernel(parts_ref, coeffs_ref, out_ref):
    sources, rows, lanes = parts_ref.shape
    sums = jnp.sum(parts_ref[...].astype(F32).reshape(sources // 2, 2, rows, lanes), axis=0)
    first, second = sums[0], sums[1]
    left = lax.broadcasted_iota(jnp.int32, first.shape, 1) < lanes // 2
    low = jnp.where(left, first, pltpu.roll(second, lanes // 2, 1))
    high = jnp.where(left, pltpu.roll(first, lanes // 2, 1), second)
    total = jnp.concatenate([low, high], axis=0)
    out_ref[...] = (coeffs_ref[...].astype(F32) + total).astype(BF16)


def local(hidden_rows, w_expand, w_contract):
    rows, width = hidden_rows.shape
    windows = lax.axis_size("seq")
    chips = windows // 2
    mine = width // chips
    project, expand, trig = window_tables(rows, windows)
    same_core = [list(range(core, windows, 2)) for core in range(2)]
    pairs = [[2 * chip, 2 * chip + 1] for chip in range(chips)]
    core = lax.axis_index("seq") % 2

    def exchange(x):
        return lax.all_to_all(x, "seq", 0, 0, axis_index_groups=same_core)

    def gather_pair(x):
        return lax.all_gather(x, "seq", axis_index_groups=pairs)

    def kernel(body, out_shape, in_specs, **rest):
        out_specs = rest.pop("out_specs", None)
        if out_specs is None:
            out_specs = jax.tree.map(lambda _: VMEM, out_shape)
        params = pltpu.CompilerParams(vmem_limit_bytes=12 << 20)
        return pl.pallas_call(
            body, out_shape=out_shape, in_specs=in_specs, out_specs=out_specs, compiler_params=params, **rest
        )

    core_index = core.astype(jnp.int32).reshape(1)
    moments, own = kernel(
        moments_kernel,
        [
            jax.ShapeDtypeStruct((width // 8, 128), F32),
            jax.ShapeDtypeStruct((2 * w_contract.shape[0], width), BF16),
        ],
        [VMEM, VMEM, ANY, ANY],
        out_specs=[VMEM, ANY],
        scratch_shapes=[pltpu.SemaphoreType.DMA((2,))],
    )(jnp.asarray(project), hidden_rows, w_expand.T, w_contract)
    received = exchange(moments.reshape(chips, -1, 128)).reshape(-1, 128)
    other_core = [(i, i ^ 1) for i in range(windows)]
    beside = lax.ppermute(own, "seq", [(i, i ^ 2) for i in range(windows)])
    across = lax.ppermute(own, "seq", other_core)
    partial = kernel(
        coeffs_kernel, jax.ShapeDtypeStruct((mine, KEEP), F32), [SMEM, VMEM, VMEM, VMEM]
    )(core_index, received, jnp.asarray(trig), jnp.asarray(expand))
    both = gather_pair(partial)
    coeffs, spread, beside = kernel(
        spread_kernel,
        [
            jax.ShapeDtypeStruct((mine, KEEP // 2), BF16),
            jax.ShapeDtypeStruct((chips, mine // 2, KEEP // 2), BF16),
            jax.ShapeDtypeStruct(beside.shape, BF16),
        ],
        [SMEM, VMEM, ANY],
        out_specs=[VMEM, VMEM, ANY],
        input_output_aliases={2: 2},
    )(core_index, both, beside)
    weights = [own, beside, across, lax.ppermute(beside, "seq", other_core)]
    branch = kernel(
        feed_forward_kernel, jax.ShapeDtypeStruct(spread.shape, BF16), [VMEM] * 5
    )(exchange(spread), *weights)
    result = kernel(add_kernel, jax.ShapeDtypeStruct(coeffs.shape, BF16), [VMEM, VMEM])(exchange(branch), coeffs)
    halves = gather_pair(result)
    halves = jnp.where(core == 0, halves[:, : mine // 2], halves[:, mine // 2 :])
    return jnp.transpose(halves, (0, 2, 1)).reshape(KEEP, mine // 2)


def solution(mesh):
    return jax.shard_map(
        local,
        mesh=mesh,
        in_specs=(P(("doc", "seq"), None), P(None, "seq"), P("seq", None)),
        out_specs=P("doc", "seq"),
        check_vma=False,
    )
```

```python
import math

import jax
import jax.numpy as jnp
import numpy as np
from jax import lax
from jax.experimental import pallas as pl
from jax.experimental.pallas import tpu as pltpu
from jax.sharding import PartitionSpec as P

KEEP = 256
MOMENTS = 16
F32, BF16 = jnp.float32, jnp.bfloat16
VMEM = pl.BlockSpec(memory_space=pltpu.VMEM)
SMEM = pl.BlockSpec(memory_space=pltpu.SMEM)
ANY = pl.BlockSpec(memory_space=pl.ANY)


def split_halves(array):
    high = np.asarray(array, np.float32).astype(jnp.bfloat16)
    low = (np.asarray(array, np.float64) - high.astype(np.float64)).astype(jnp.bfloat16)
    return high, low


def window_tables(rows, windows):
    t = (2.0 * np.arange(rows) + 1.0 - rows) / rows
    basis, _ = np.linalg.qr(np.polynomial.chebyshev.chebvander(t, MOMENTS - 1))
    basis = basis[:, list(range(0, MOMENTS, 2)) + list(range(1, MOMENTS, 2))]
    k = np.arange(KEEP)
    inner = np.pi * np.outer(k, t) / (2 * windows)
    norm = math.sqrt(2.0 / (rows * windows))
    even = norm * np.cos(inner) @ basis[:, : MOMENTS // 2]
    odd = -norm * np.sin(inner) @ basis[:, MOMENTS // 2 :]
    expand = np.concatenate([even, odd], axis=1).T.astype(np.float32)
    high, low = split_halves(basis.T)
    project = np.concatenate([high, low], axis=0)
    theta = np.pi * np.outer(2 * np.arange(windows) + 1, k) / (2 * windows)
    trig = np.concatenate([np.cos(theta), np.sin(theta)], axis=1)
    trig = trig.reshape(windows // 2, 2, 2 * KEEP).transpose(1, 0, 2)
    high, low = split_halves(trig)
    return project, expand, np.concatenate([high, low, high, low], axis=1)


def moments_kernel(project_hbm, rows_hbm, out_ref, project_ref, held, loaded):
    steps, _, columns = held.shape
    first = pltpu.make_async_copy(project_hbm, project_ref, loaded.at[steps])
    loads = [
        pltpu.make_async_copy(rows_hbm.at[:, pl.ds(step * columns, columns)], held.at[step], loaded.at[step])
        for step in range(steps)
    ]
    for copy in [first] + loads:
        copy.start()
    row = lax.broadcasted_iota(jnp.int32, (128, 128), 0) % 8
    lane = lax.broadcasted_iota(jnp.int32, (128, 128), 1) // MOMENTS
    first.wait()
    project = project_ref[...]
    for step in range(steps):
        loads[step].wait()
        both = jnp.dot(project, held[step], preferred_element_type=F32)
        moments = both[:MOMENTS] + both[MOMENTS:]
        spread = jnp.concatenate([moments] * 8, axis=0)
        for block in range(columns // 128):
            turned = spread[:, 128 * block : 128 * (block + 1)].T
            packed = jnp.where(row == lane, turned, 0.0).reshape(16, 8, 128).sum(axis=1)
            top = step * columns // 8 + 16 * block
            out_ref[top : top + 16, :] = packed


def coeffs_kernel(core_ref, moments_ref, trig_ref, expand_ref, out_ref):
    trig = trig_ref[core_ref[0]]
    sources = trig.shape[0] // 4
    expand = expand_ref[...]
    half = MOMENTS // 2
    for part in range(4):
        rows = moments_ref[pl.ds(part, sources, stride=4), :]
        high = rows.astype(BF16)
        low = (rows - high.astype(F32)).astype(BF16)
        stacked = jnp.concatenate([high, high, low, low], axis=0)
        turned = lax.dot_general(stacked, trig, (((0,), (0,)), ((), ())), preferred_element_type=F32)
        even = turned[:, :KEEP].reshape(8, MOMENTS, KEEP)[:, :half]
        odd = turned[:, KEEP:].reshape(8, MOMENTS, KEEP)[:, half:]
        out_ref[8 * part : 8 * (part + 1), :] = (even * expand[:half] + odd * expand[half:]).sum(axis=1)


def spread_kernel(core_ref, both_ref, coeffs_ref, out_ref):
    total = both_ref[0] + both_ref[1]
    half = total.shape[1] // 2
    mine = jnp.where(core_ref[0] == 0, total[:, :half], total[:, half:])
    coeffs_ref[...] = jnp.where(core_ref[0] == 0, total[:16], total[16:]).astype(BF16)
    low, high = mine[:16], mine[16:]
    left = lax.broadcasted_iota(jnp.int32, low.shape, 1) < half // 2
    first = jnp.where(left, low, pltpu.roll(high, half // 2, 1)).astype(BF16)
    second = jnp.where(left, pltpu.roll(low, half // 2, 1), high).astype(BF16)
    pair = jnp.stack([first, second])
    out_ref[...] = jnp.broadcast_to(pair[None], (out_ref.shape[0] // 2,) + pair.shape).reshape(out_ref.shape)


def feed_forward_kernel(coeffs_ref, *refs):
    weights, out_ref = refs[:-1], refs[-1]
    packed = coeffs_ref[...]
    kept = packed.shape[2] // 2
    width = packed.shape[0] * 32
    coeffs = jnp.concatenate([packed[:, :, :kept], packed[:, :, kept:]], axis=1).reshape(width, kept)
    wide = coeffs.astype(F32)
    scale = lax.rsqrt(jnp.sum(wide * wide, axis=0, keepdims=True) / width + 1e-06)
    branch = jnp.zeros((kept, width), F32)
    for expand_ref, contract_ref in zip(weights[::2], weights[1::2]):
        expanded = jnp.dot(expand_ref[...], coeffs, preferred_element_type=F32) * scale
        activated = jax.nn.gelu(expanded).T.astype(BF16)
        branch += jnp.dot(activated, contract_ref[...], preferred_element_type=F32)
    for block in range(width // 128):
        turned = branch[:, 128 * block : 128 * (block + 1)].T.reshape(8, 16, kept)
        out_ref[8 * block : 8 * (block + 1)] = jnp.concatenate([turned[:, :8], turned[:, 8:]], axis=2).astype(BF16)


def add_kernel(parts_ref, coeffs_ref, out_ref):
    sources, rows, lanes = parts_ref.shape
    sums = jnp.sum(parts_ref[...].astype(F32).reshape(sources // 4, 4, rows, lanes), axis=0)
    left = lax.broadcasted_iota(jnp.int32, (rows, lanes), 1) < lanes // 2
    for core in range(2):
        first, second = sums[core], sums[2 + core]
        low = jnp.where(left, first, pltpu.roll(second, lanes // 2, 1))
        high = jnp.where(left, pltpu.roll(first, lanes // 2, 1), second)
        total = jnp.concatenate([low, high], axis=0)
        columns = pl.ds(lanes * core, lanes)
        out_ref[:, columns] = (coeffs_ref[:, columns].astype(F32) + total).astype(BF16)


def local(hidden_rows, w_expand, w_contract):
    rows, width = hidden_rows.shape
    windows = lax.axis_size("seq")
    chips = windows // 2
    mine = width // chips
    project, expand, trig = window_tables(rows, windows)
    same_core = [list(range(core, windows, 2)) for core in range(2)]
    pairs = [[2 * chip, 2 * chip + 1] for chip in range(chips)]
    core = lax.axis_index("seq") % 2

    def exchange(x):
        return lax.all_to_all(x, "seq", 0, 0, axis_index_groups=same_core)

    def gather_pair(x):
        return lax.all_gather(x, "seq", axis_index_groups=pairs)

    def kernel(body, out_shape, in_specs, vmem=12, **rest):
        out_specs = rest.pop("out_specs", None)
        if out_specs is None:
            out_specs = jax.tree.map(lambda _: VMEM, out_shape)
        params = pltpu.CompilerParams(vmem_limit_bytes=vmem << 20)
        return pl.pallas_call(
            body, out_shape=out_shape, in_specs=in_specs, out_specs=out_specs, compiler_params=params, **rest
        )

    core_index = core.astype(jnp.int32).reshape(1)
    moments = kernel(
        moments_kernel,
        jax.ShapeDtypeStruct((width // 8, 128), F32),
        [ANY, ANY],
        vmem=60,
        scratch_shapes=[
            pltpu.VMEM(project.shape, BF16),
            pltpu.VMEM((2, rows, width // 2), BF16),
            pltpu.SemaphoreType.DMA((3,)),
        ],
    )(jnp.asarray(project), hidden_rows)
    received = exchange(moments.reshape(chips, -1, 128)).reshape(-1, 128)
    beside = [(i, i ^ 2) for i in range(windows)]
    w_expand = w_expand.T
    weights = [w_expand, w_contract, lax.ppermute(w_expand, "seq", beside), lax.ppermute(w_contract, "seq", beside)]
    weights = [gather_pair(x).reshape(-1, width) for x in weights]
    partial = kernel(
        coeffs_kernel, jax.ShapeDtypeStruct((mine, KEEP), F32), [SMEM, VMEM, VMEM, VMEM]
    )(core_index, received, jnp.asarray(trig), jnp.asarray(expand))
    both = gather_pair(partial)
    coeffs, spread = kernel(
        spread_kernel,
        [
            jax.ShapeDtypeStruct((mine // 2, KEEP), BF16),
            jax.ShapeDtypeStruct((chips, mine // 2, KEEP // 2), BF16),
        ],
        [SMEM, VMEM],
    )(core_index, both)
    branch = kernel(
        feed_forward_kernel, jax.ShapeDtypeStruct((windows, mine // 4, KEEP // 2), BF16), [VMEM] * 5
    )(exchange(spread), *weights)
    parts = lax.all_to_all(branch, "seq", 0, 0)
    return kernel(add_kernel, jax.ShapeDtypeStruct(coeffs.shape, BF16), [VMEM, VMEM])(parts, coeffs).T


def solution(mesh):
    return jax.shard_map(
        local,
        mesh=mesh,
        in_specs=(P(("doc", "seq"), None), P(None, "seq"), P("seq", None)),
        out_specs=P("doc", "seq"),
        check_vma=False,
    )
```

```python
import math

import jax
import jax.numpy as jnp
import numpy as np
from jax import lax
from jax.experimental import pallas as pl
from jax.experimental.pallas import tpu as pltpu
from jax.sharding import PartitionSpec as P

KEEP = 256
TURN = 36
MOMENTS = 16
F32, BF16 = jnp.float32, jnp.bfloat16
VMEM = pl.BlockSpec(memory_space=pltpu.VMEM)
SMEM = pl.BlockSpec(memory_space=pltpu.SMEM)
ANY = pl.BlockSpec(memory_space=pl.ANY)


def split_halves(array):
    high = np.asarray(array, np.float32).astype(jnp.bfloat16)
    low = (np.asarray(array, np.float64) - high.astype(np.float64)).astype(jnp.bfloat16)
    return high, low


def window_tables(rows, windows, turn):
    t = (2.0 * np.arange(rows) + 1.0 - rows) / rows
    basis, _ = np.linalg.qr(np.polynomial.chebyshev.chebvander(t, MOMENTS - 1))
    basis = basis[:, list(range(0, MOMENTS, 2)) + list(range(1, MOMENTS, 2))]
    k = np.arange(KEEP)
    inner = np.pi * np.outer(k, t) / (2 * windows)
    norm = math.sqrt(2.0 / (rows * windows))
    even = norm * np.cos(inner) @ basis[:, : MOMENTS // 2]
    odd = -norm * np.sin(inner) @ basis[:, MOMENTS // 2 :]
    expand = np.concatenate([even, odd], axis=1).T.astype(np.float32)
    high, low = split_halves(basis.T)
    project = np.concatenate([high, low], axis=0)
    theta = np.pi * np.outer(2 * np.arange(windows) + 1, k) / (2 * windows)
    trig = np.concatenate([np.cos(theta), np.sin(theta)], axis=1)
    trig = np.roll(trig.reshape(windows // 2, 2, 2 * KEEP), -turn, axis=0).transpose(1, 0, 2)
    high, low = split_halves(trig)
    return project, expand, np.concatenate([high, low, high, low], axis=1)


def moments_kernel(project_hbm, rows_hbm, out_ref, project_ref, held, loaded):
    steps, _, columns = held.shape
    first = pltpu.make_async_copy(project_hbm, project_ref, loaded.at[steps])
    loads = [
        pltpu.make_async_copy(rows_hbm.at[:, pl.ds(step * columns, columns)], held.at[step], loaded.at[step])
        for step in range(steps)
    ]
    for copy in [first] + loads:
        copy.start()
    row = lax.broadcasted_iota(jnp.int32, (128, 128), 0) % 8
    lane = lax.broadcasted_iota(jnp.int32, (128, 128), 1) // MOMENTS
    first.wait()
    project = project_ref[...]
    for step in range(steps):
        loads[step].wait()
        both = jnp.dot(project, held[step], preferred_element_type=F32)
        moments = both[:MOMENTS] + both[MOMENTS:]
        spread = jnp.concatenate([moments] * 8, axis=0)
        for block in range(columns // 128):
            turned = spread[:, 128 * block : 128 * (block + 1)].T
            packed = jnp.where(row == lane, turned, 0.0).reshape(16, 8, 128).sum(axis=1)
            top = (step * columns // 8 + 16 * block - 4 * TURN) % out_ref.shape[0]
            out_ref[top : top + 16, :] = packed


def coeffs_kernel(core_ref, moments_ref, trig_ref, expand_ref, out_ref):
    trig = trig_ref[core_ref[0]]
    sources = trig.shape[0] // 4
    expand = expand_ref[...]
    half = MOMENTS // 2
    for part in range(4):
        rows = moments_ref[pl.ds(part, sources, stride=4), :]
        high = rows.astype(BF16)
        low = (rows - high.astype(F32)).astype(BF16)
        stacked = jnp.concatenate([high, high, low, low], axis=0)
        turned = lax.dot_general(stacked, trig, (((0,), (0,)), ((), ())), preferred_element_type=F32)
        even = turned[:, :KEEP].reshape(8, MOMENTS, KEEP)[:, :half]
        odd = turned[:, KEEP:].reshape(8, MOMENTS, KEEP)[:, half:]
        out_ref[8 * part : 8 * (part + 1), :] = (even * expand[:half] + odd * expand[half:]).sum(axis=1)


def spread_kernel(core_ref, both_ref, coeffs_ref, out_ref):
    total = both_ref[0] + both_ref[1]
    half = total.shape[1] // 2
    mine = jnp.where(core_ref[0] == 0, total[:, :half], total[:, half:])
    coeffs_ref[...] = jnp.where(core_ref[0] == 0, total[:16], total[16:]).astype(BF16)
    low, high = mine[:16], mine[16:]
    left = lax.broadcasted_iota(jnp.int32, low.shape, 1) < half // 2
    first = jnp.where(left, low, pltpu.roll(high, half // 2, 1)).astype(BF16)
    second = jnp.where(left, pltpu.roll(low, half // 2, 1), high).astype(BF16)
    pair = jnp.stack([first, second])
    out_ref[...] = jnp.broadcast_to(pair[None], (out_ref.shape[0] // 2,) + pair.shape).reshape(out_ref.shape)


def feed_forward_kernel(coeffs_ref, *refs):
    weights, out_ref = refs[:-1], refs[-1]
    packed = coeffs_ref[...]
    packed = jnp.concatenate([packed[-TURN:], packed[:-TURN]], axis=0)
    kept = packed.shape[2] // 2
    width = packed.shape[0] * 32
    coeffs = jnp.concatenate([packed[:, :, :kept], packed[:, :, kept:]], axis=1).reshape(width, kept)
    wide = coeffs.astype(F32)
    scale = lax.rsqrt(jnp.sum(wide * wide, axis=0, keepdims=True) / width + 1e-06)
    branch = jnp.zeros((kept, width), F32)
    for expand_ref, contract_ref in zip(weights[::2], weights[1::2]):
        expanded = jnp.dot(expand_ref[...], coeffs, preferred_element_type=F32) * scale
        activated = jax.nn.gelu(expanded).T.astype(BF16)
        branch += jnp.dot(activated, contract_ref[...], preferred_element_type=F32)
    for block in range(width // 128):
        turned = branch[:, 128 * block : 128 * (block + 1)].T.reshape(8, 16, kept)
        first = (8 * block - 2 * TURN) % out_ref.shape[0]
        out_ref[first : first + 8] = jnp.concatenate([turned[:, :8], turned[:, 8:]], axis=2).astype(BF16)


def add_kernel(parts_ref, coeffs_ref, out_ref):
    sources, rows, lanes = parts_ref.shape
    sums = jnp.sum(parts_ref[...].astype(F32).reshape(sources // 4, 4, rows, lanes), axis=0)
    left = lax.broadcasted_iota(jnp.int32, (rows, lanes), 1) < lanes // 2
    for core in range(2):
        first, second = sums[core], sums[2 + core]
        low = jnp.where(left, first, pltpu.roll(second, lanes // 2, 1))
        high = jnp.where(left, pltpu.roll(first, lanes // 2, 1), second)
        total = jnp.concatenate([low, high], axis=0)
        columns = pl.ds(lanes * core, lanes)
        out_ref[:, columns] = (coeffs_ref[:, columns].astype(F32) + total).astype(BF16)


def local(hidden_rows, w_expand, w_contract):
    rows, width = hidden_rows.shape
    windows = lax.axis_size("seq")
    chips = windows // 2
    mine = width // chips
    project, expand, trig = window_tables(rows, windows, TURN)
    pairs = [[2 * chip, 2 * chip + 1] for chip in range(chips)]
    core = lax.axis_index("seq") % 2

    def exchange(x, step=2):
        groups = [[(2 * TURN + i) % windows for i in range(core, windows, step)] for core in range(step)]
        return lax.all_to_all(x, "seq", 0, 0, axis_index_groups=groups)

    def gather_pair(x):
        return lax.all_gather(x, "seq", axis_index_groups=pairs)

    def kernel(body, out_shape, in_specs, vmem=12, **rest):
        out_specs = rest.pop("out_specs", None)
        if out_specs is None:
            out_specs = jax.tree.map(lambda _: VMEM, out_shape)
        params = pltpu.CompilerParams(vmem_limit_bytes=vmem << 20)
        return pl.pallas_call(
            body, out_shape=out_shape, in_specs=in_specs, out_specs=out_specs, compiler_params=params, **rest
        )

    core_index = core.astype(jnp.int32).reshape(1)
    moments = kernel(
        moments_kernel,
        jax.ShapeDtypeStruct((width // 8, 128), F32),
        [ANY, ANY],
        vmem=60,
        scratch_shapes=[
            pltpu.VMEM(project.shape, BF16),
            pltpu.VMEM((2, rows, width // 2), BF16),
            pltpu.SemaphoreType.DMA((3,)),
        ],
    )(jnp.asarray(project), hidden_rows)
    received = exchange(moments.reshape(chips, -1, 128)).reshape(-1, 128)
    beside = [(i, i ^ 2) for i in range(windows)]
    w_expand = w_expand.T
    weights = [w_expand, w_contract, lax.ppermute(w_expand, "seq", beside), lax.ppermute(w_contract, "seq", beside)]
    weights = [gather_pair(x).reshape(-1, width) for x in weights]
    partial = kernel(
        coeffs_kernel, jax.ShapeDtypeStruct((mine, KEEP), F32), [SMEM, VMEM, VMEM, VMEM]
    )(core_index, received, jnp.asarray(trig), jnp.asarray(expand))
    both = gather_pair(partial)
    coeffs, spread = kernel(
        spread_kernel,
        [
            jax.ShapeDtypeStruct((mine // 2, KEEP), BF16),
            jax.ShapeDtypeStruct((chips, mine // 2, KEEP // 2), BF16),
        ],
        [SMEM, VMEM],
    )(core_index, both)
    branch = kernel(
        feed_forward_kernel, jax.ShapeDtypeStruct((windows, mine // 4, KEEP // 2), BF16), [VMEM] * 5
    )(exchange(spread), *weights)
    parts = exchange(branch, step=1)
    return kernel(add_kernel, jax.ShapeDtypeStruct(coeffs.shape, BF16), [VMEM, VMEM])(parts, coeffs).T


def solution(mesh):
    return jax.shard_map(
        local,
        mesh=mesh,
        in_specs=(P(("doc", "seq"), None), P(None, "seq"), P("seq", None)),
        out_specs=P("doc", "seq"),
        check_vma=False,
    )
```

```python
import math

import jax
import jax.numpy as jnp
import numpy as np
from jax import lax
from jax.experimental import pallas as pl
from jax.experimental.pallas import tpu as pltpu
from jax.sharding import PartitionSpec as P

KEEP = 256
TURN = 36
MOMENTS = 16
F32, BF16 = jnp.float32, jnp.bfloat16
VMEM = pl.BlockSpec(memory_space=pltpu.VMEM)
SMEM = pl.BlockSpec(memory_space=pltpu.SMEM)
ANY = pl.BlockSpec(memory_space=pl.ANY)


def split_halves(array):
    high = np.asarray(array, np.float32).astype(jnp.bfloat16)
    low = (np.asarray(array, np.float64) - high.astype(np.float64)).astype(jnp.bfloat16)
    return high, low


def window_tables(rows, windows, turn):
    t = (2.0 * np.arange(rows) + 1.0 - rows) / rows
    basis, _ = np.linalg.qr(np.polynomial.chebyshev.chebvander(t, MOMENTS - 1))
    basis = basis[:, list(range(0, MOMENTS, 2)) + list(range(1, MOMENTS, 2))]
    k = np.arange(KEEP)
    inner = np.pi * np.outer(k, t) / (2 * windows)
    norm = math.sqrt(2.0 / (rows * windows))
    even = norm * np.cos(inner) @ basis[:, : MOMENTS // 2]
    odd = -norm * np.sin(inner) @ basis[:, MOMENTS // 2 :]
    expand = np.concatenate([even, odd], axis=1).T.astype(np.float32)
    high, low = split_halves(basis.T)
    project = np.concatenate([high, low], axis=0)
    theta = np.pi * np.outer(2 * np.arange(windows) + 1, k) / (2 * windows)
    trig = np.concatenate([np.cos(theta), np.sin(theta)], axis=1)
    trig = np.roll(trig.reshape(windows // 2, 2, 2 * KEEP), -turn, axis=0).transpose(1, 0, 2)
    high, low = split_halves(trig)
    return project, expand, np.concatenate([high, low, high, low], axis=1)


def moments_kernel(project_hbm, rows_hbm, out_ref, project_ref, held, loaded):
    steps, _, columns = held.shape
    first = pltpu.make_async_copy(project_hbm, project_ref, loaded.at[steps])
    loads = [
        pltpu.make_async_copy(rows_hbm.at[:, pl.ds(step * columns, columns)], held.at[step], loaded.at[step])
        for step in range(steps)
    ]
    for copy in [first] + loads:
        copy.start()
    row = lax.broadcasted_iota(jnp.int32, (128, 128), 0) % 8
    lane = lax.broadcasted_iota(jnp.int32, (128, 128), 1) // MOMENTS
    first.wait()
    project = project_ref[...]
    for step in range(steps):
        loads[step].wait()
        both = jnp.dot(project, held[step], preferred_element_type=F32)
        moments = both[:MOMENTS] + both[MOMENTS:]
        spread = jnp.concatenate([moments] * 8, axis=0)
        for block in range(columns // 128):
            turned = spread[:, 128 * block : 128 * (block + 1)].T
            packed = jnp.where(row == lane, turned, 0.0).reshape(16, 8, 128).sum(axis=1)
            top = (step * columns // 8 + 16 * block - 4 * TURN) % out_ref.shape[0]
            out_ref[top : top + 16, :] = packed


def coeffs_kernel(core_ref, moments_ref, trig_ref, expand_ref, out_ref):
    trig = trig_ref[core_ref[0]]
    sources = trig.shape[0] // 4
    expand = expand_ref[...]
    half = MOMENTS // 2
    for part in range(4):
        rows = moments_ref[pl.ds(part, sources, stride=4), :]
        high = rows.astype(BF16)
        low = (rows - high.astype(F32)).astype(BF16)
        stacked = jnp.concatenate([high, high, low, low], axis=0)
        turned = lax.dot_general(stacked, trig, (((0,), (0,)), ((), ())), preferred_element_type=F32)
        even = turned[:, :KEEP].reshape(8, MOMENTS, KEEP)[:, :half]
        odd = turned[:, KEEP:].reshape(8, MOMENTS, KEEP)[:, half:]
        out_ref[8 * part : 8 * (part + 1), :] = (even * expand[:half] + odd * expand[half:]).sum(axis=1)


def spread_kernel(core_ref, both_ref, coeffs_ref, out_ref):
    total = both_ref[0] + both_ref[1]
    half = total.shape[1] // 2
    mine = jnp.where(core_ref[0] == 0, total[:, :half], total[:, half:])
    coeffs_ref[...] = jnp.where(core_ref[0] == 0, total[:16], total[16:]).astype(BF16)
    low, high = mine[:16], mine[16:]
    left = lax.broadcasted_iota(jnp.int32, low.shape, 1) < half // 2
    first = jnp.where(left, low, pltpu.roll(high, half // 2, 1)).astype(BF16)
    second = jnp.where(left, pltpu.roll(low, half // 2, 1), high).astype(BF16)
    pair = jnp.stack([first, second])
    out_ref[...] = jnp.broadcast_to(pair[None], (out_ref.shape[0] // 2,) + pair.shape).reshape(out_ref.shape)


def stack_kernel(expand_ref, contract_ref, out_ref):
    units = expand_ref.shape[0]
    out_ref[:units, :] = expand_ref[...]
    out_ref[units:, :] = contract_ref[...]


def scale_kernel(packed_ref, scale_ref):
    wide = packed_ref[...].astype(F32)
    sums = jnp.sum(wide * wide, axis=(0, 1))[None]
    lanes = sums.shape[1]
    sums += pltpu.roll(sums, lanes // 2, 1)
    scale_ref[...] = lax.rsqrt(sums / (wide.size // (lanes // 2)) + 1e-06)


def feed_forward_kernel(packed_ref, scale_ref, *refs):
    weights, out_ref = refs[:-1], refs[-1]
    units = weights[0].shape[0] // 2
    packed = jnp.concatenate([packed_ref[-TURN:], packed_ref[:-TURN]], axis=0)
    kept = packed.shape[2] // 2
    width = packed.shape[0] * 32
    coeffs = jnp.concatenate([packed[:, :, :kept], packed[:, :, kept:]], axis=1).reshape(width, kept)
    expand = jnp.concatenate([ref[:units, :] for ref in weights], axis=0)
    expanded = jnp.dot(expand, coeffs, preferred_element_type=F32) * scale_ref[:, :kept]
    activated = jax.nn.gelu(expanded).T.astype(BF16)
    for start in range(0, width, 256):
        contract = jnp.concatenate([ref[units:, start : start + 256] for ref in weights], axis=0)
        branch = jnp.dot(activated, contract, preferred_element_type=F32)
        for half in range(2):
            turned = branch[:, 128 * half : 128 * (half + 1)].T.reshape(8, 16, kept)
            first = (start // 16 + 8 * half - 2 * TURN) % out_ref.shape[0]
            out_ref[first : first + 8] = jnp.concatenate([turned[:, :8], turned[:, 8:]], axis=2).astype(BF16)


def add_kernel(parts_ref, coeffs_ref, out_ref):
    sources, rows, lanes = parts_ref.shape
    sums = jnp.sum(parts_ref[...].astype(F32).reshape(sources // 4, 4, rows, lanes), axis=0)
    left = lax.broadcasted_iota(jnp.int32, (rows, lanes), 1) < lanes // 2
    for core in range(2):
        first, second = sums[core], sums[2 + core]
        low = jnp.where(left, first, pltpu.roll(second, lanes // 2, 1))
        high = jnp.where(left, pltpu.roll(first, lanes // 2, 1), second)
        total = jnp.concatenate([low, high], axis=0)
        columns = pl.ds(lanes * core, lanes)
        out_ref[:, columns] = (coeffs_ref[:, columns].astype(F32) + total).astype(BF16)


def local(hidden_rows, w_expand, w_contract):
    rows, width = hidden_rows.shape
    windows = lax.axis_size("seq")
    chips = windows // 2
    mine = width // chips
    project, expand, trig = window_tables(rows, windows, TURN)
    pairs = [[2 * chip, 2 * chip + 1] for chip in range(chips)]
    core = lax.axis_index("seq") % 2

    def exchange(x, step=2):
        groups = [[(2 * TURN + i) % windows for i in range(core, windows, step)] for core in range(step)]
        return lax.all_to_all(x, "seq", 0, 0, axis_index_groups=groups)

    def gather_pair(x):
        return lax.all_gather(x, "seq", axis_index_groups=pairs)

    def kernel(body, out_shape, in_specs, vmem=12, **rest):
        out_specs = rest.pop("out_specs", None)
        if out_specs is None:
            out_specs = jax.tree.map(lambda _: VMEM, out_shape)
        params = pltpu.CompilerParams(vmem_limit_bytes=vmem << 20)
        return pl.pallas_call(
            body, out_shape=out_shape, in_specs=in_specs, out_specs=out_specs, compiler_params=params, **rest
        )

    core_index = core.astype(jnp.int32).reshape(1)
    moments = kernel(
        moments_kernel,
        jax.ShapeDtypeStruct((width // 8, 128), F32),
        [ANY, ANY],
        vmem=60,
        scratch_shapes=[
            pltpu.VMEM(project.shape, BF16),
            pltpu.VMEM((2, rows, width // 2), BF16),
            pltpu.SemaphoreType.DMA((3,)),
        ],
    )(jnp.asarray(project), hidden_rows)
    received = exchange(moments.reshape(chips, -1, 128)).reshape(-1, 128)
    own = kernel(
        stack_kernel, jax.ShapeDtypeStruct((2 * w_contract.shape[0], width), BF16), [VMEM, VMEM]
    )(w_expand.T, w_contract)
    beside = lax.ppermute(own, "seq", [(i, i ^ 2) for i in range(windows)])
    other_core = [(i, i ^ 1) for i in range(windows)]
    weights = [own, beside, lax.ppermute(own, "seq", other_core), lax.ppermute(beside, "seq", other_core)]
    partial = kernel(
        coeffs_kernel, jax.ShapeDtypeStruct((mine, KEEP), F32), [SMEM, VMEM, VMEM, VMEM]
    )(core_index, received, jnp.asarray(trig), jnp.asarray(expand))
    both = gather_pair(partial)
    coeffs, spread = kernel(
        spread_kernel,
        [
            jax.ShapeDtypeStruct((mine // 2, KEEP), BF16),
            jax.ShapeDtypeStruct((chips, mine // 2, KEEP // 2), BF16),
        ],
        [SMEM, VMEM],
    )(core_index, both)
    gathered = exchange(spread)
    scale = kernel(
        scale_kernel,
        jax.ShapeDtypeStruct((1, KEEP // 2), F32),
        [VMEM],
        cost_estimate=pl.CostEstimate(flops=2 * 10**10, bytes_accessed=1 << 20, transcendentals=0),
    )(gathered)
    branch = kernel(
        feed_forward_kernel, jax.ShapeDtypeStruct((windows, mine // 4, KEEP // 2), BF16), [VMEM] * 6
    )(gathered, scale, *weights)
    parts = exchange(branch, step=1)
    return kernel(add_kernel, jax.ShapeDtypeStruct(coeffs.shape, BF16), [VMEM, VMEM])(parts, coeffs).T


def solution(mesh):
    return jax.shard_map(
        local,
        mesh=mesh,
        in_specs=(P(("doc", "seq"), None), P(None, "seq"), P("seq", None)),
        out_specs=P("doc", "seq"),
        check_vma=False,
    )
```

```python
import math

import jax
import jax.numpy as jnp
import numpy as np
from jax import lax
from jax.experimental import pallas as pl
from jax.experimental.pallas import tpu as pltpu
from jax.sharding import PartitionSpec as P

KEEP = 256
TURN = 36
MOMENTS = 16
F32, BF16 = jnp.float32, jnp.bfloat16
VMEM = pl.BlockSpec(memory_space=pltpu.VMEM)
SMEM = pl.BlockSpec(memory_space=pltpu.SMEM)
ANY = pl.BlockSpec(memory_space=pl.ANY)


def split_halves(array):
    high = np.asarray(array, np.float32).astype(jnp.bfloat16)
    low = (np.asarray(array, np.float64) - high.astype(np.float64)).astype(jnp.bfloat16)
    return high, low


def window_tables(rows, windows, turn):
    t = (2.0 * np.arange(rows) + 1.0 - rows) / rows
    basis, _ = np.linalg.qr(np.polynomial.chebyshev.chebvander(t, MOMENTS - 1))
    basis = basis[:, list(range(0, MOMENTS, 2)) + list(range(1, MOMENTS, 2))]
    k = np.arange(KEEP)
    inner = np.pi * np.outer(k, t) / (2 * windows)
    norm = math.sqrt(2.0 / (rows * windows))
    even = norm * np.cos(inner) @ basis[:, : MOMENTS // 2]
    odd = -norm * np.sin(inner) @ basis[:, MOMENTS // 2 :]
    expand = np.concatenate([even, odd], axis=1).T.astype(np.float32)
    high, low = split_halves(basis.T)
    project = np.concatenate([high, low], axis=0)
    theta = np.pi * np.outer(2 * np.arange(windows) + 1, k) / (2 * windows)
    trig = np.concatenate([np.cos(theta), np.sin(theta)], axis=1)
    trig = np.roll(trig.reshape(windows // 2, 2, 2 * KEEP), -turn, axis=0).transpose(1, 0, 2)
    high, low = split_halves(trig)
    return project, expand, np.concatenate([high, low, high, low], axis=1)


def moments_kernel(project_hbm, rows_hbm, out_ref, project_ref, held, loaded):
    steps, _, columns = held.shape
    first = pltpu.make_async_copy(project_hbm, project_ref, loaded.at[steps])
    loads = [
        pltpu.make_async_copy(rows_hbm.at[:, pl.ds(step * columns, columns)], held.at[step], loaded.at[step])
        for step in range(steps)
    ]
    for copy in [first] + loads:
        copy.start()
    row = lax.broadcasted_iota(jnp.int32, (128, 128), 0) % 8
    lane = lax.broadcasted_iota(jnp.int32, (128, 128), 1) // MOMENTS
    first.wait()
    project = project_ref[...]
    for step in range(steps):
        loads[step].wait()
        both = jnp.dot(project, held[step], preferred_element_type=F32)
        moments = both[:MOMENTS] + both[MOMENTS:]
        spread = jnp.concatenate([moments] * 8, axis=0)
        for block in range(columns // 128):
            turned = spread[:, 128 * block : 128 * (block + 1)].T
            packed = jnp.where(row == lane, turned, 0.0).reshape(16, 8, 128).sum(axis=1)
            top = (step * columns // 8 + 16 * block - 4 * TURN) % out_ref.shape[0]
            out_ref[top : top + 16, :] = packed


def coeffs_kernel(core_ref, moments_ref, trig_ref, expand_ref, out_ref):
    trig = trig_ref[core_ref[0]]
    sources = trig.shape[0] // 4
    expand = expand_ref[...]
    half = MOMENTS // 2
    for part in range(4):
        rows = moments_ref[pl.ds(part, sources, stride=4), :]
        high = rows.astype(BF16)
        low = (rows - high.astype(F32)).astype(BF16)
        stacked = jnp.concatenate([high, high, low, low], axis=0)
        turned = lax.dot_general(stacked, trig, (((0,), (0,)), ((), ())), preferred_element_type=F32)
        even = turned[:, :KEEP].reshape(8, MOMENTS, KEEP)[:, :half]
        odd = turned[:, KEEP:].reshape(8, MOMENTS, KEEP)[:, half:]
        out_ref[8 * part : 8 * (part + 1), :] = (even * expand[:half] + odd * expand[half:]).sum(axis=1)


def spread_kernel(core_ref, both_ref, coeffs_ref, out_ref):
    total = both_ref[0] + both_ref[1]
    half = total.shape[1] // 2
    mine = jnp.where(core_ref[0] == 0, total[:, :half], total[:, half:])
    coeffs_ref[...] = jnp.where(core_ref[0] == 0, total[:16], total[16:]).astype(BF16)
    low, high = mine[:16], mine[16:]
    left = lax.broadcasted_iota(jnp.int32, low.shape, 1) < half // 2
    first = jnp.where(left, low, pltpu.roll(high, half // 2, 1)).astype(BF16)
    second = jnp.where(left, pltpu.roll(low, half // 2, 1), high).astype(BF16)
    pair = jnp.stack([first, second])
    out_ref[...] = jnp.broadcast_to(pair[None], (out_ref.shape[0] // 2,) + pair.shape).reshape(out_ref.shape)


def stack_kernel(expand_ref, contract_ref, out_ref):
    units = expand_ref.shape[0]
    out_ref[:units, :] = expand_ref[...]
    out_ref[units:, :] = contract_ref[...]


def scale_kernel(packed_ref, scale_ref):
    wide = packed_ref[...].astype(F32)
    sums = jnp.sum(wide * wide, axis=(0, 1))[None]
    lanes = sums.shape[1]
    sums += pltpu.roll(sums, lanes // 2, 1)
    scale_ref[...] = lax.rsqrt(sums / (wide.size // (lanes // 2)) + 1e-06)


def feed_forward_kernel(packed_ref, scale_ref, *refs):
    weights, out_ref = refs[:-1], refs[-1]
    units = weights[0].shape[0] // 2
    packed = jnp.concatenate([packed_ref[-TURN:], packed_ref[:-TURN]], axis=0)
    kept = packed.shape[2] // 2
    width = packed.shape[0] * 32
    coeffs = jnp.concatenate([packed[:, :, :kept], packed[:, :, kept:]], axis=1).reshape(width, kept)
    expand = jnp.concatenate([ref[:units, :] for ref in weights], axis=0)
    expanded = jnp.dot(expand, coeffs, preferred_element_type=F32) * scale_ref[:, :kept]
    activated = jax.nn.gelu(expanded).T.astype(BF16)
    for start in range(0, width, 256):
        contract = jnp.concatenate([ref[units:, start : start + 256] for ref in weights], axis=0)
        branch = jnp.dot(activated, contract, preferred_element_type=F32).astype(BF16)
        for half in range(2):
            turned = branch[:, 128 * half : 128 * (half + 1)].T.reshape(4, 2, 16, kept)
            turned = jnp.stack([turned[:, 1], turned[:, 0]], axis=1).reshape(8, 16, kept)
            first = (start // 16 + 8 * half - 2 * TURN) % out_ref.shape[0]
            out_ref[first : first + 8] = jnp.concatenate([turned[:, :8], turned[:, 8:]], axis=2)


def add_kernel(parts_ref, coeffs_ref, out_ref):
    sources, rows, lanes = parts_ref.shape
    sums = jnp.sum(parts_ref[...].astype(F32).reshape(sources // 4, 4, rows, lanes), axis=0)
    left = lax.broadcasted_iota(jnp.int32, (rows, lanes), 1) < lanes // 2
    for core in range(2):
        first, second = sums[1 - core], sums[3 - core]
        low = jnp.where(left, first, pltpu.roll(second, lanes // 2, 1))
        high = jnp.where(left, pltpu.roll(first, lanes // 2, 1), second)
        total = jnp.concatenate([low, high], axis=0)
        columns = pl.ds(lanes * core, lanes)
        out_ref[:, columns] = (coeffs_ref[:, columns].astype(F32) + total).astype(BF16)


def local(hidden_rows, w_expand, w_contract):
    rows, width = hidden_rows.shape
    windows = lax.axis_size("seq")
    chips = windows // 2
    mine = width // chips
    project, expand, trig = window_tables(rows, windows, TURN)
    pairs = [[2 * chip, 2 * chip + 1] for chip in range(chips)]
    core = lax.axis_index("seq") % 2

    same_core = [[(2 * TURN + i) % windows for i in range(core, windows, 2)] for core in range(2)]
    both_cores = [[(2 * TURN + i) % windows ^ 1 for i in range(windows)]]

    def exchange(x, groups=same_core):
        return lax.all_to_all(x, "seq", 0, 0, axis_index_groups=groups)

    def gather_pair(x):
        return lax.all_gather(x, "seq", axis_index_groups=pairs)

    def kernel(body, out_shape, in_specs, vmem=12, **rest):
        out_specs = rest.pop("out_specs", None)
        if out_specs is None:
            out_specs = jax.tree.map(lambda _: VMEM, out_shape)
        params = pltpu.CompilerParams(vmem_limit_bytes=vmem << 20)
        return pl.pallas_call(
            body, out_shape=out_shape, in_specs=in_specs, out_specs=out_specs, compiler_params=params, **rest
        )

    core_index = core.astype(jnp.int32).reshape(1)
    moments = kernel(
        moments_kernel,
        jax.ShapeDtypeStruct((width // 8, 128), F32),
        [ANY, ANY],
        vmem=60,
        scratch_shapes=[
            pltpu.VMEM(project.shape, BF16),
            pltpu.VMEM((2, rows, width // 2), BF16),
            pltpu.SemaphoreType.DMA((3,)),
        ],
    )(jnp.asarray(project), hidden_rows)
    received = exchange(moments.reshape(chips, -1, 128)).reshape(-1, 128)
    own = kernel(
        stack_kernel, jax.ShapeDtypeStruct((2 * w_contract.shape[0], width), BF16), [VMEM, VMEM]
    )(w_expand.T, w_contract)
    beside = lax.ppermute(own, "seq", [(i, i ^ 2) for i in range(windows)])
    other_core = [(i, i ^ 1) for i in range(windows)]
    weights = [own, beside, lax.ppermute(own, "seq", other_core), lax.ppermute(beside, "seq", other_core)]
    partial = kernel(
        coeffs_kernel, jax.ShapeDtypeStruct((mine, KEEP), F32), [SMEM, VMEM, VMEM, VMEM]
    )(core_index, received, jnp.asarray(trig), jnp.asarray(expand))
    both = gather_pair(partial)
    coeffs, spread = kernel(
        spread_kernel,
        [
            jax.ShapeDtypeStruct((mine // 2, KEEP), BF16),
            jax.ShapeDtypeStruct((chips, mine // 2, KEEP // 2), BF16),
        ],
        [SMEM, VMEM],
    )(core_index, both)
    gathered = exchange(spread)
    scale = kernel(
        scale_kernel,
        jax.ShapeDtypeStruct((1, KEEP // 2), F32),
        [VMEM],
        cost_estimate=pl.CostEstimate(flops=2 * 10**10, bytes_accessed=1 << 20, transcendentals=0),
    )(gathered)
    branch = kernel(
        feed_forward_kernel, jax.ShapeDtypeStruct((windows, mine // 4, KEEP // 2), BF16), [VMEM] * 6
    )(gathered, scale, *weights)
    parts = exchange(branch, both_cores)
    return kernel(add_kernel, jax.ShapeDtypeStruct(coeffs.shape, BF16), [VMEM, VMEM])(parts, coeffs).T


def solution(mesh):
    return jax.shard_map(
        local,
        mesh=mesh,
        in_specs=(P(("doc", "seq"), None), P(None, "seq"), P("seq", None)),
        out_specs=P("doc", "seq"),
        check_vma=False,
    )
```

```python
import math

import jax
import jax.numpy as jnp
import numpy as np
from jax import lax
from jax.experimental import pallas as pl
from jax.experimental.pallas import tpu as pltpu
from jax.sharding import PartitionSpec as P

KEEP = 256
TURN = 36
MOMENTS = 16
F32, BF16 = jnp.float32, jnp.bfloat16
VMEM = pl.BlockSpec(memory_space=pltpu.VMEM)
SMEM = pl.BlockSpec(memory_space=pltpu.SMEM)
ANY = pl.BlockSpec(memory_space=pl.ANY)


def group_order(chips, group):
    return [(TURN + i) % chips ^ (1 - group) for i in range(chips)]


def split_halves(array):
    high = np.asarray(array, np.float32).astype(jnp.bfloat16)
    low = (np.asarray(array, np.float64) - high.astype(np.float64)).astype(jnp.bfloat16)
    return high, low


def window_tables(rows, windows):
    t = (2.0 * np.arange(rows) + 1.0 - rows) / rows
    basis, _ = np.linalg.qr(np.polynomial.chebyshev.chebvander(t, MOMENTS - 1))
    basis = basis[:, list(range(0, MOMENTS, 2)) + list(range(1, MOMENTS, 2))]
    k = np.arange(KEEP)
    inner = np.pi * np.outer(k, t) / (2 * windows)
    norm = math.sqrt(2.0 / (rows * windows))
    even = norm * np.cos(inner) @ basis[:, : MOMENTS // 2]
    odd = -norm * np.sin(inner) @ basis[:, MOMENTS // 2 :]
    expand = np.concatenate([even, odd], axis=1).T.astype(np.float32)
    high, low = split_halves(basis.T)
    project = np.concatenate([high, low], axis=0)
    theta = np.pi * np.outer(2 * np.arange(windows) + 1, k) / (2 * windows)
    trig = np.concatenate([np.cos(theta), np.sin(theta)], axis=1)
    orders = [group_order(windows // 2, group) for group in range(2)]
    rows_of = [[2 * chip + (chip % 2 ^ group) for chip in order] for group, order in enumerate(orders)]
    trig = trig[np.asarray(rows_of)]
    high, low = split_halves(trig)
    return project, expand, np.concatenate([high, low, high, low], axis=1)


def moments_kernel(group_ref, project_hbm, rows_hbm, out_ref, project_ref, held, loaded):
    steps, count, columns = held.shape
    first = pltpu.make_async_copy(project_hbm, project_ref, loaded.at[steps])
    loads = [
        pltpu.make_async_copy(rows_hbm.at[pl.ds(step * count, count)], held.at[step], loaded.at[step])
        for step in range(steps)
    ]
    for copy in [first] + loads:
        copy.start()
    row = lax.broadcasted_iota(jnp.int32, (128, 128), 0) % 8
    lane = lax.broadcasted_iota(jnp.int32, (128, 128), 1) // MOMENTS
    first.wait()
    both = jnp.zeros((2 * MOMENTS, columns), F32)
    for step in range(steps):
        loads[step].wait()
        part = project_ref[:, step * count : (step + 1) * count]
        both += jnp.dot(part, held[step], preferred_element_type=F32)
    moments = both[:MOMENTS] + both[MOMENTS:]
    spread = jnp.concatenate([moments] * 8, axis=0)
    for block in range(columns // 128):
        turned = spread[:, 128 * block : 128 * (block + 1)].T
        packed = jnp.where(row == lane, turned, 0.0).reshape(16, 8, 128).sum(axis=1)
        pairs = packed.reshape(2, 2, 4, 128)
        swapped = jnp.stack([pairs[:, 1], pairs[:, 0]], axis=1).reshape(16, 128)
        top = (16 * block - 4 * TURN) % out_ref.shape[0]
        out_ref[top : top + 16, :] = jnp.where(group_ref[0] == 0, swapped, packed)


def coeffs_kernel(group_ref, moments_ref, trig_ref, expand_ref, out_ref):
    trig = trig_ref[group_ref[0]]
    sources = trig.shape[0] // 4
    expand = expand_ref[...]
    half = MOMENTS // 2
    for part in range(4):
        rows = moments_ref[pl.ds(part, sources, stride=4), :]
        high = rows.astype(BF16)
        low = (rows - high.astype(F32)).astype(BF16)
        stacked = jnp.concatenate([high, high, low, low], axis=0)
        turned = lax.dot_general(stacked, trig, (((0,), (0,)), ((), ())), preferred_element_type=F32)
        even = turned[:, :KEEP].reshape(8, MOMENTS, KEEP)[:, :half]
        odd = turned[:, KEEP:].reshape(8, MOMENTS, KEEP)[:, half:]
        out_ref[8 * part : 8 * (part + 1), :] = (even * expand[:half] + odd * expand[half:]).sum(axis=1)


def spread_kernel(core_ref, group_ref, both_ref, coeffs_ref, out_ref):
    total = both_ref[0] + both_ref[1]
    half = total.shape[1] // 2
    coeffs_ref[...] = jnp.where(core_ref[0] == 0, total[:16], total[16:]).astype(BF16)
    left = lax.broadcasted_iota(jnp.int32, (16, half), 1) < half // 2

    def quarter(core, parity):
        low, high = total[:16, half * core : half * (core + 1)], total[16:, half * core : half * (core + 1)]
        even = jnp.where(left, low, pltpu.roll(high, half // 2, 1))
        odd = jnp.where(left, pltpu.roll(low, half // 2, 1), high)
        return jnp.where(parity == 0, even, odd).astype(BF16)

    pair = jnp.stack([quarter(1, 1 - group_ref[0]), quarter(0, group_ref[0])])
    out_ref[...] = jnp.broadcast_to(pair[None], (out_ref.shape[0] // 2,) + pair.shape).reshape(out_ref.shape)


def stack_kernel(expand_ref, contract_ref, out_ref):
    units = expand_ref.shape[0]
    out_ref[:units, :] = expand_ref[...]
    out_ref[units:, :] = contract_ref[...]


def scale_kernel(packed_ref, scale_ref):
    wide = packed_ref[...].astype(F32)
    sums = jnp.sum(wide * wide, axis=(0, 1))[None]
    lanes = sums.shape[1]
    sums += pltpu.roll(sums, lanes // 2, 1)
    scale_ref[...] = lax.rsqrt(sums / (wide.size // (lanes // 2)) + 1e-06)


def feed_forward_kernel(group_ref, packed_ref, scale_ref, *refs):
    weights, out_ref = refs[:-1], refs[-1]
    units = weights[0].shape[0] // 2
    packed = jnp.concatenate([packed_ref[-TURN:], packed_ref[:-TURN]], axis=0)
    pairs = packed.reshape((packed.shape[0] // 2, 2) + packed.shape[1:])
    swapped = jnp.stack([pairs[:, 1], pairs[:, 0]], axis=1).reshape(packed.shape)
    packed = jnp.where(group_ref[0] == 0, swapped, packed)
    kept = packed.shape[2] // 2
    width = packed.shape[0] * 32
    coeffs = jnp.concatenate([packed[:, :, :kept], packed[:, :, kept:]], axis=1).reshape(width, kept)
    expand = jnp.concatenate([ref[:units, :] for ref in weights], axis=0)
    expanded = jnp.dot(expand, coeffs, preferred_element_type=F32) * scale_ref[:, :kept]
    activated = jax.nn.gelu(expanded).T.astype(BF16)
    for start in range(0, width, 256):
        contract = jnp.concatenate([ref[units:, start : start + 256] for ref in weights], axis=0)
        branch = jnp.dot(activated, contract, preferred_element_type=F32).astype(BF16)
        for half in range(2):
            turned = branch[:, 128 * half : 128 * (half + 1)].T.reshape(4, 2, 16, kept)
            turned = jnp.stack([turned[:, 1], turned[:, 0]], axis=1).reshape(8, 16, kept)
            first = (start // 16 + 8 * half - 2 * TURN) % out_ref.shape[0]
            out_ref[first : first + 8] = jnp.concatenate([turned[:, :8], turned[:, 8:]], axis=2)


def add_kernel(parts_ref, coeffs_ref, out_ref):
    sources, rows, lanes = parts_ref.shape
    sums = jnp.sum(parts_ref[...].astype(F32).reshape(sources // 4, 4, rows, lanes), axis=0)
    left = lax.broadcasted_iota(jnp.int32, (rows, lanes), 1) < lanes // 2
    for core in range(2):
        first, second = sums[1 - core], sums[3 - core]
        low = jnp.where(left, first, pltpu.roll(second, lanes // 2, 1))
        high = jnp.where(left, pltpu.roll(first, lanes // 2, 1), second)
        total = jnp.concatenate([low, high], axis=0)
        columns = pl.ds(lanes * core, lanes)
        out_ref[:, columns] = (coeffs_ref[:, columns].astype(F32) + total).astype(BF16)


def local(hidden_rows, w_expand, w_contract):
    rows, width = hidden_rows.shape
    windows = lax.axis_size("seq")
    chips = windows // 2
    mine = width // chips
    project, expand, trig = window_tables(rows, windows)
    pairs = [[2 * chip, 2 * chip + 1] for chip in range(chips)]
    core = lax.axis_index("seq") % 2

    mixed = [[2 * chip + (chip % 2 ^ group) for chip in group_order(chips, group)] for group in range(2)]
    both_cores = [[(2 * TURN + i) % windows ^ 1 for i in range(windows)]]

    def exchange(x, groups=mixed):
        return lax.all_to_all(x, "seq", 0, 0, axis_index_groups=groups)

    def gather_pair(x):
        return lax.all_gather(x, "seq", axis_index_groups=pairs)

    def kernel(body, out_shape, in_specs, vmem=12, **rest):
        out_specs = rest.pop("out_specs", None)
        if out_specs is None:
            out_specs = jax.tree.map(lambda _: VMEM, out_shape)
        params = pltpu.CompilerParams(vmem_limit_bytes=vmem << 20)
        return pl.pallas_call(
            body, out_shape=out_shape, in_specs=in_specs, out_specs=out_specs, compiler_params=params, **rest
        )

    core_index = core.astype(jnp.int32).reshape(1)
    group_index = ((lax.axis_index("seq") // 2 + core) % 2).astype(jnp.int32).reshape(1)
    moments = kernel(
        moments_kernel,
        jax.ShapeDtypeStruct((width // 8, 128), F32),
        [SMEM, ANY, ANY],
        vmem=60,
        scratch_shapes=[
            pltpu.VMEM(project.shape, BF16),
            pltpu.VMEM((4, rows // 4, width), BF16),
            pltpu.SemaphoreType.DMA((5,)),
        ],
    )(group_index, jnp.asarray(project), hidden_rows)
    received = exchange(moments.reshape(chips, -1, 128)).reshape(-1, 128)
    own = kernel(
        stack_kernel, jax.ShapeDtypeStruct((2 * w_contract.shape[0], width), BF16), [VMEM, VMEM]
    )(w_expand.T, w_contract)
    beside = lax.ppermute(own, "seq", [(i, i ^ 2) for i in range(windows)])
    other_core = [(i, i ^ 1) for i in range(windows)]
    weights = [own, beside, lax.ppermute(own, "seq", other_core), lax.ppermute(beside, "seq", other_core)]
    partial = kernel(
        coeffs_kernel, jax.ShapeDtypeStruct((mine, KEEP), F32), [SMEM, VMEM, VMEM, VMEM]
    )(group_index, received, jnp.asarray(trig), jnp.asarray(expand))
    both = gather_pair(partial)
    coeffs, spread = kernel(
        spread_kernel,
        [
            jax.ShapeDtypeStruct((mine // 2, KEEP), BF16),
            jax.ShapeDtypeStruct((chips, mine // 2, KEEP // 2), BF16),
        ],
        [SMEM, SMEM, VMEM],
    )(core_index, group_index, both)
    gathered = exchange(spread)
    scale = kernel(
        scale_kernel,
        jax.ShapeDtypeStruct((1, KEEP // 2), F32),
        [VMEM],
        cost_estimate=pl.CostEstimate(flops=2 * 10**10, bytes_accessed=1 << 20, transcendentals=0),
    )(gathered)
    branch = kernel(
        feed_forward_kernel, jax.ShapeDtypeStruct((windows, mine // 4, KEEP // 2), BF16), [SMEM] + [VMEM] * 6
    )(group_index, gathered, scale, *weights)
    parts = exchange(branch, both_cores)
    return kernel(add_kernel, jax.ShapeDtypeStruct(coeffs.shape, BF16), [VMEM, VMEM])(parts, coeffs).T


def solution(mesh):
    return jax.shard_map(
        local,
        mesh=mesh,
        in_specs=(P(("doc", "seq"), None), P(None, "seq"), P("seq", None)),
        out_specs=P("doc", "seq"),
        check_vma=False,
    )
```

```python
import math

import jax
import jax.numpy as jnp
import numpy as np
from jax import lax
from jax.experimental import pallas as pl
from jax.experimental.pallas import tpu as pltpu
from jax.sharding import PartitionSpec as P

KEEP = 256
TURN = 36
MOMENTS = 16
F32, BF16 = jnp.float32, jnp.bfloat16
VMEM = pl.BlockSpec(memory_space=pltpu.VMEM)
SMEM = pl.BlockSpec(memory_space=pltpu.SMEM)
ANY = pl.BlockSpec(memory_space=pl.ANY)


def group_order(chips, group):
    return [(TURN + i) % chips ^ (1 - group) for i in range(chips)]


def split_halves(array):
    high = np.asarray(array, np.float32).astype(jnp.bfloat16)
    low = (np.asarray(array, np.float64) - high.astype(np.float64)).astype(jnp.bfloat16)
    return high, low


def window_tables(rows, windows):
    t = (2.0 * np.arange(rows) + 1.0 - rows) / rows
    basis, _ = np.linalg.qr(np.polynomial.chebyshev.chebvander(t, MOMENTS - 1))
    basis = basis[:, list(range(0, MOMENTS, 2)) + list(range(1, MOMENTS, 2))]
    k = np.arange(KEEP)
    inner = np.pi * np.outer(k, t) / (2 * windows)
    norm = math.sqrt(2.0 / (rows * windows))
    even = norm * np.cos(inner) @ basis[:, : MOMENTS // 2]
    odd = -norm * np.sin(inner) @ basis[:, MOMENTS // 2 :]
    expand = np.concatenate([even, odd], axis=1).T.astype(np.float32)
    high, low = split_halves(basis.T)
    project = np.concatenate([high, low], axis=0)
    theta = np.pi * np.outer(2 * np.arange(windows) + 1, k) / (2 * windows)
    trig = np.concatenate([np.cos(theta), np.sin(theta)], axis=1)
    orders = [group_order(windows // 2, group) for group in range(2)]
    rows_of = [[2 * chip + (chip % 2 ^ group) for chip in order] for group, order in enumerate(orders)]
    trig = trig[np.asarray(rows_of)]
    high, low = split_halves(trig)
    return project, expand, np.concatenate([high, low, high, low], axis=1)


def moments_kernel(group_ref, project_hbm, rows_hbm, out_ref, project_ref, held, loaded):
    count, columns = held.shape
    blocks = [slice(0, count // 2), slice(count // 2, 3 * count // 4), slice(3 * count // 4, count)]
    first = pltpu.make_async_copy(project_hbm, project_ref, loaded.at[len(blocks)])
    loads = [
        pltpu.make_async_copy(rows_hbm.at[block], held.at[block], loaded.at[step]) for step, block in enumerate(blocks)
    ]
    for copy in [first] + loads:
        copy.start()
    row = lax.broadcasted_iota(jnp.int32, (128, 128), 0) % 8
    lane = lax.broadcasted_iota(jnp.int32, (128, 128), 1) // MOMENTS
    first.wait()
    both = jnp.zeros((2 * MOMENTS, columns), F32)
    for load, block in zip(loads, blocks):
        load.wait()
        both += jnp.dot(project_ref[:, block], held[block], preferred_element_type=F32)
    moments = both[:MOMENTS] + both[MOMENTS:]
    spread = jnp.concatenate([moments] * 8, axis=0)
    for block in range(columns // 128):
        turned = spread[:, 128 * block : 128 * (block + 1)].T
        packed = jnp.where(row == lane, turned, 0.0).reshape(16, 8, 128).sum(axis=1)
        pairs = packed.reshape(2, 2, 4, 128)
        swapped = jnp.stack([pairs[:, 1], pairs[:, 0]], axis=1).reshape(16, 128)
        top = (16 * block - 4 * TURN) % out_ref.shape[0]
        out_ref[top : top + 16, :] = jnp.where(group_ref[0] == 0, swapped, packed)


def coeffs_kernel(group_ref, moments_ref, trig_ref, expand_ref, out_ref):
    trig = trig_ref[group_ref[0]]
    sources = trig.shape[0] // 4
    expand = expand_ref[...]
    half = MOMENTS // 2
    for part in range(4):
        rows = moments_ref[pl.ds(part, sources, stride=4), :]
        high = rows.astype(BF16)
        low = (rows - high.astype(F32)).astype(BF16)
        stacked = jnp.concatenate([high, high, low, low], axis=0)
        turned = lax.dot_general(stacked, trig, (((0,), (0,)), ((), ())), preferred_element_type=F32)
        even = turned[:, :KEEP].reshape(8, MOMENTS, KEEP)[:, :half]
        odd = turned[:, KEEP:].reshape(8, MOMENTS, KEEP)[:, half:]
        out_ref[8 * part : 8 * (part + 1), :] = (even * expand[:half] + odd * expand[half:]).sum(axis=1)


def spread_kernel(core_ref, group_ref, both_ref, coeffs_ref, out_ref):
    total = both_ref[0] + both_ref[1]
    half = total.shape[1] // 2
    coeffs_ref[...] = jnp.where(core_ref[0] == 0, total[:16], total[16:]).astype(BF16)
    left = lax.broadcasted_iota(jnp.int32, (16, half), 1) < half // 2

    def quarter(core, parity):
        low, high = total[:16, half * core : half * (core + 1)], total[16:, half * core : half * (core + 1)]
        even = jnp.where(left, low, pltpu.roll(high, half // 2, 1))
        odd = jnp.where(left, pltpu.roll(low, half // 2, 1), high)
        return jnp.where(parity == 0, even, odd).astype(BF16)

    pair = jnp.stack([quarter(1, 1 - group_ref[0]), quarter(0, group_ref[0])])
    out_ref[...] = jnp.broadcast_to(pair[None], (out_ref.shape[0] // 2,) + pair.shape).reshape(out_ref.shape)


def stack_kernel(expand_ref, contract_ref, out_ref):
    units = expand_ref.shape[0]
    out_ref[:units, :] = expand_ref[...]
    out_ref[units:, :] = contract_ref[...]


def scale_kernel(packed_ref, scale_ref):
    wide = packed_ref[...].astype(F32)
    sums = jnp.sum(wide * wide, axis=(0, 1))[None]
    lanes = sums.shape[1]
    sums += pltpu.roll(sums, lanes // 2, 1)
    scale_ref[...] = lax.rsqrt(sums / (wide.size // (lanes // 2)) + 1e-06)


def feed_forward_kernel(group_ref, packed_ref, scale_ref, *refs):
    weights, out_ref = refs[:-1], refs[-1]
    units = weights[0].shape[0] // 2
    packed = jnp.concatenate([packed_ref[-TURN:], packed_ref[:-TURN]], axis=0)
    pairs = packed.reshape((packed.shape[0] // 2, 2) + packed.shape[1:])
    swapped = jnp.stack([pairs[:, 1], pairs[:, 0]], axis=1).reshape(packed.shape)
    packed = jnp.where(group_ref[0] == 0, swapped, packed)
    kept = packed.shape[2] // 2
    width = packed.shape[0] * 32
    coeffs = jnp.concatenate([packed[:, :, :kept], packed[:, :, kept:]], axis=1).reshape(width, kept)
    expand = jnp.concatenate([ref[:units, :] for ref in weights], axis=0)
    expanded = jnp.dot(expand, coeffs, preferred_element_type=F32) * scale_ref[:, :kept]
    activated = jax.nn.gelu(expanded).T.astype(BF16)
    for start in range(0, width, 256):
        contract = jnp.concatenate([ref[units:, start : start + 256] for ref in weights], axis=0)
        branch = jnp.dot(activated, contract, preferred_element_type=F32).astype(BF16)
        for half in range(2):
            turned = branch[:, 128 * half : 128 * (half + 1)].T.reshape(4, 2, 16, kept)
            turned = jnp.stack([turned[:, 1], turned[:, 0]], axis=1).reshape(8, 16, kept)
            first = (start // 16 + 8 * half - 2 * TURN) % out_ref.shape[0]
            out_ref[first : first + 8] = jnp.concatenate([turned[:, :8], turned[:, 8:]], axis=2)


def add_kernel(parts_ref, coeffs_ref, out_ref):
    sources, rows, lanes = parts_ref.shape
    sums = jnp.sum(parts_ref[...].astype(F32).reshape(sources // 4, 4, rows, lanes), axis=0)
    left = lax.broadcasted_iota(jnp.int32, (rows, lanes), 1) < lanes // 2
    for core in range(2):
        first, second = sums[1 - core], sums[3 - core]
        low = jnp.where(left, first, pltpu.roll(second, lanes // 2, 1))
        high = jnp.where(left, pltpu.roll(first, lanes // 2, 1), second)
        total = jnp.concatenate([low, high], axis=0)
        columns = pl.ds(lanes * core, lanes)
        out_ref[:, columns] = (coeffs_ref[:, columns].astype(F32) + total).astype(BF16)


def local(hidden_rows, w_expand, w_contract):
    rows, width = hidden_rows.shape
    windows = lax.axis_size("seq")
    chips = windows // 2
    mine = width // chips
    project, expand, trig = window_tables(rows, windows)
    pairs = [[2 * chip, 2 * chip + 1] for chip in range(chips)]
    core = lax.axis_index("seq") % 2

    mixed = [[2 * chip + (chip % 2 ^ group) for chip in group_order(chips, group)] for group in range(2)]
    both_cores = [[(2 * TURN + i) % windows ^ 1 for i in range(windows)]]

    def exchange(x, groups=mixed):
        return lax.all_to_all(x, "seq", 0, 0, axis_index_groups=groups)

    def gather_pair(x):
        return lax.all_gather(x, "seq", axis_index_groups=pairs)

    def kernel(body, out_shape, in_specs, vmem=12, **rest):
        out_specs = rest.pop("out_specs", None)
        if out_specs is None:
            out_specs = jax.tree.map(lambda _: VMEM, out_shape)
        params = pltpu.CompilerParams(vmem_limit_bytes=vmem << 20)
        return pl.pallas_call(
            body, out_shape=out_shape, in_specs=in_specs, out_specs=out_specs, compiler_params=params, **rest
        )

    core_index = core.astype(jnp.int32).reshape(1)
    group_index = ((lax.axis_index("seq") // 2 + core) % 2).astype(jnp.int32).reshape(1)
    moments = kernel(
        moments_kernel,
        jax.ShapeDtypeStruct((width // 8, 128), F32),
        [SMEM, ANY, ANY],
        vmem=60,
        scratch_shapes=[
            pltpu.VMEM(project.shape, BF16),
            pltpu.VMEM((rows, width), BF16),
            pltpu.SemaphoreType.DMA((4,)),
        ],
    )(group_index, jnp.asarray(project), hidden_rows)
    received = exchange(moments.reshape(chips, -1, 128)).reshape(-1, 128)
    own = kernel(
        stack_kernel, jax.ShapeDtypeStruct((2 * w_contract.shape[0], width), BF16), [VMEM, VMEM]
    )(w_expand.T, w_contract)
    beside = lax.ppermute(own, "seq", [(i, i ^ 2) for i in range(windows)])
    other_core = [(i, i ^ 1) for i in range(windows)]
    weights = [own, beside, lax.ppermute(own, "seq", other_core), lax.ppermute(beside, "seq", other_core)]
    partial = kernel(
        coeffs_kernel, jax.ShapeDtypeStruct((mine, KEEP), F32), [SMEM, VMEM, VMEM, VMEM]
    )(group_index, received, jnp.asarray(trig), jnp.asarray(expand))
    both = gather_pair(partial)
    coeffs, spread = kernel(
        spread_kernel,
        [
            jax.ShapeDtypeStruct((mine // 2, KEEP), BF16),
            jax.ShapeDtypeStruct((chips, mine // 2, KEEP // 2), BF16),
        ],
        [SMEM, SMEM, VMEM],
    )(core_index, group_index, both)
    gathered = exchange(spread)
    scale = kernel(
        scale_kernel,
        jax.ShapeDtypeStruct((1, KEEP // 2), F32),
        [VMEM],
        cost_estimate=pl.CostEstimate(flops=2 * 10**10, bytes_accessed=1 << 20, transcendentals=0),
    )(gathered)
    branch = kernel(
        feed_forward_kernel, jax.ShapeDtypeStruct((windows, mine // 4, KEEP // 2), BF16), [SMEM] + [VMEM] * 6
    )(group_index, gathered, scale, *weights)
    parts = exchange(branch, both_cores)
    return kernel(add_kernel, jax.ShapeDtypeStruct(coeffs.shape, BF16), [VMEM, VMEM])(parts, coeffs).T


def solution(mesh):
    return jax.shard_map(
        local,
        mesh=mesh,
        in_specs=(P(("doc", "seq"), None), P(None, "seq"), P("seq", None)),
        out_specs=P("doc", "seq"),
        check_vma=False,
    )
```
